32 devices in a mesh: expert: 8 (over z, y), dp: 4 (over x, core).
Axes of the slice: x: 2, y: 2, z: 4, core: 2. Of those that a mesh axis runs over, the one named last changes fastest.
Arguments:
- inputs: bfloat16 [4096, 1024], P(('expert', 'dp')), may hold values from -6 to 6
- out_grad: bfloat16 [4096, 1024], P(('expert', 'dp')), may hold values from -6 to 6
- expert_ids: int32 [4096, 2], P(('expert', 'dp')), may hold values from 0 to 7, as said below
- slot_ids: int32 [4096, 2], P(('expert', 'dp')), may hold values from -1 to 31, as said below
- gate_values: bfloat16 [4096, 2], P(('expert', 'dp')), may hold values from 0.099609375 to 0.8984375
- first_layer: bfloat16 [8, 1024, 4096], P('expert', None, 'dp'), may hold values from -0.1875 to 0.1875
- second_layer: bfloat16 [8, 4096, 1024], P('expert', 'dp'), may hold values from -0.09375 to 0.09375
Outputs:
- input_grad: bfloat16 [4096, 1024], P(('expert', 'dp'))
- gate_grad: bfloat16 [4096, 2], P(('expert', 'dp'))
- first_grad: bfloat16 [8, 1024, 4096], P('expert', None, 'dp')
- second_grad: bfloat16 [8, 4096, 1024], P('expert', 'dp')
The draws below stay inside these ranges and needn't reach their ends.
Inputs may be any that keep to these rules, and one draw needn't show every extreme that they name: `expert_ids`: the two experts of a token differ. slot_ids[t, k] is the number of assignments to expert expert_ids[t, k] from the token's group that come before it, where all first assignments of the group come before all second ones, in token order; it is -1 where that number is 32 or more. No two kept assignments of a group share an expert and a slot.
All inputs are finite; a program needn't handle non-finite values.
Results may differ from the reference program's by a relative error of at most 0.008.
Values may be sent and summed in bfloat16 or wider, within the bound.
A program may use at most 128 MiB of HBM per device.

```python
import math
import jax
import jax.numpy as jnp
from jax import lax

D = 1024
H = 4096
TOK_DEV = 128
EXPERTS = 8
CAP = 32
TOKENS = 4096


def routing(key):
    subkeys = jax.random.split(key, 4)
    lowest = jnp.minimum(jax.random.randint(subkeys[0], (TOKENS,), 0, EXPERTS), jax.random.randint(subkeys[1], (TOKENS,), 0, EXPERTS))
    shuffle = jax.random.permutation(subkeys[2], EXPERTS)
    primary = shuffle[lowest]
    secondary = (primary + jax.random.randint(subkeys[3], (TOKENS,), 1, EXPERTS)) % EXPERTS
    group_count = TOKENS // TOK_DEV
    picks = jnp.concatenate([primary.reshape(group_count, TOK_DEV), secondary.reshape(group_count, TOK_DEV)], axis=1)
    matches = (picks[:, :, None] == jnp.arange(EXPERTS, dtype=jnp.int32)).astype(jnp.int32)
    ranking = jnp.sum((jnp.cumsum(matches, axis=1) - 1) * matches, axis=2)
    slot_rank = jnp.where(ranking < 2 * TOK_DEV // EXPERTS, ranking, -1)
    slot_pair = jnp.stack([slot_rank[:, :TOK_DEV], slot_rank[:, TOK_DEV:]], axis=2).reshape(TOKENS, 2)
    expert_pair = jnp.stack([primary, secondary], axis=1)
    return (expert_pair.astype(jnp.int32), slot_pair.astype(jnp.int32))


def draw_expert_ids(key, part):
    expert_pair, slot_pair = routing(key)
    return expert_pair


def draw_slot_ids(key, part):
    expert_pair, slot_pair = routing(key)
    return slot_pair


def block_levels(own_key, dims, cuts, least, high):
    factor_of, own = 1.0, jax.random.fold_in(own_key, 6)
    for dim, shards_of in cuts:
        steps = jnp.exp(jax.random.uniform(jax.random.fold_in(own, dim), (shards_of,), jnp.float32, least / len(cuts), high / len(cuts)))
        factor_of = factor_of * jnp.repeat(steps, dims[dim] // shards_of).reshape([-1 if axis == dim else 1 for axis in range(len(dims))])
    return factor_of


def noise(own_key, shape, scale, most, cuts=(), kind=jnp.bfloat16):
    gain = block_levels(own_key, shape, cuts, -0.22, 0.18) if cuts else 1.0
    result = jax.random.normal(own_key, shape, jnp.float32) * scale * gain
    return jnp.minimum(jnp.maximum(result, -most), most).astype(kind)


def setup_inputs(seed: int = 0) -> dict:
    seeds = jax.random.split(jax.random.key(seed), 8)
    return {
        "inputs": noise(seeds[0], (TOKENS, D), 1.0, 6.0, ((0, 32),)),
        "out_grad": noise(seeds[1], (TOKENS, D), 1.0, 6.0, ((0, 32),)),
        "expert_ids": draw_expert_ids(jax.random.fold_in(seeds[7], 71), 0),
        "slot_ids": draw_slot_ids(jax.random.fold_in(seeds[7], 71), 0),
        "gate_values": jnp.clip(0.099609375 + 0.7988281 * jax.random.uniform(seeds[4], (TOKENS, 2), jnp.float32) ** block_levels(seeds[4], (TOKENS, 2), ((0, 32),), -0.2, 0.2), 0.099609375, 0.8984375).astype(jnp.bfloat16),
        "first_layer": noise(seeds[5], (EXPERTS, D, H), D ** -0.5, 0.1875, ((0, 8), (2, 4))),
        "second_layer": noise(seeds[6], (EXPERTS, H, D), H ** -0.5, 0.09375, ((0, 8), (1, 4))),
    }


coef_root = math.sqrt(2.0 / math.pi)

def gelu_pair(pre_value):
    cubic_term = 0.044715 * pre_value * pre_value * pre_value
    tanh_part = jnp.tanh(coef_root * (pre_value + cubic_term))
    activation = 0.5 * pre_value * (1.0 + tanh_part)
    derivative = 0.5 * (1.0 + tanh_part) + 0.5 * pre_value * (1.0 - tanh_part * tanh_part) * coef_root * (1.0 + 3.0 * 0.044715 * pre_value * pre_value)
    return (activation, derivative)

def slot_tables(expert_ids, slot_ids, gate_values, experts, capacity):
    tok_count = expert_ids.shape[0]
    position = jnp.where(slot_ids >= 0, expert_ids * capacity + slot_ids, experts * capacity).astype(jnp.int32)
    flat_slots = position.reshape(-1)
    owners = jnp.repeat(jnp.arange(tok_count, dtype=jnp.int32), expert_ids.shape[1])
    owner_table = jnp.full((experts * capacity,), tok_count, jnp.int32).at[flat_slots].set(owners, mode='drop')
    gate_table = jnp.zeros((experts * capacity,), gate_values.dtype).at[flat_slots].set(gate_values.reshape(-1), mode='drop')
    return (position, owner_table, gate_table)

def take_rows(source, index):
    return jnp.take(source, index, axis=0, mode='fill', fill_value=0)

def reference(inputs, out_grad, expert_ids, slot_ids, gate_values, first_layer, second_layer):
    group_count = TOKENS // TOK_DEV
    in_groups = inputs.reshape(group_count, TOK_DEV, D)
    cot_groups = out_grad.reshape(group_count, TOK_DEV, D)
    id_groups = expert_ids.reshape(group_count, TOK_DEV, 2)
    slot_groups = slot_ids.reshape(group_count, TOK_DEV, 2)
    gate_groups = gate_values.reshape(group_count, TOK_DEV, 2)
    position, owner_table, gate_table = jax.vmap(lambda first_arg, second_arg, third_arg: slot_tables(first_arg, second_arg, third_arg, EXPERTS, CAP))(id_groups, slot_groups, gate_groups)
    dispatched = jax.vmap(take_rows)(in_groups, owner_table)
    cotangent = jax.vmap(take_rows)(cot_groups, owner_table)
    dispatched = dispatched.reshape(group_count, EXPERTS, CAP, D).transpose(1, 0, 2, 3).reshape(EXPERTS, group_count * CAP, D)
    cotangent = cotangent.reshape(group_count, EXPERTS, CAP, D).transpose(1, 0, 2, 3).reshape(EXPERTS, group_count * CAP, D)
    gate_slots = gate_table.reshape(group_count, EXPERTS, CAP).transpose(1, 0, 2).reshape(EXPERTS, group_count * CAP)

    def per_expert(operands):
        slot_in, slot_cot, slot_gate, layer_in, layer_out = operands
        pre = jnp.dot(slot_in, layer_in, preferred_element_type=jnp.float32)
        act_full, derivative = gelu_pair(pre)
        activation = act_full.astype(jnp.bfloat16)
        back = lax.dot_general(slot_cot, layer_out, (((1,), (1,)), ((), ())), preferred_element_type=jnp.float32)
        inner_dot = lax.optimization_barrier(jnp.sum(activation.astype(jnp.float32) * back, axis=1))
        gate_col = slot_gate.astype(jnp.float32)[:, None]
        scaled = (gate_col * slot_cot.astype(jnp.float32)).astype(jnp.bfloat16)
        hidden_grad = (gate_col * back * derivative).astype(jnp.bfloat16)
        in_grad = lax.dot_general(slot_in, hidden_grad, (((0,), (0,)), ((), ())), preferred_element_type=jnp.float32).astype(jnp.bfloat16)
        out_grad_w = lax.dot_general(activation, scaled, (((0,), (0,)), ((), ())), preferred_element_type=jnp.float32).astype(jnp.bfloat16)
        slot_grad = lax.dot_general(hidden_grad, layer_in, (((1,), (1,)), ((), ())), preferred_element_type=jnp.float32).astype(jnp.bfloat16)
        return (slot_grad, inner_dot.astype(jnp.bfloat16), in_grad, out_grad_w)
    slot_grad, slot_inner, first_grad, second_grad = lax.map(per_expert, (dispatched, cotangent, gate_slots, first_layer, second_layer))
    slot_grad = slot_grad.reshape(EXPERTS, group_count, CAP, D).transpose(1, 0, 2, 3).reshape(group_count, EXPERTS * CAP, D)
    slot_inner = slot_inner.reshape(EXPERTS, group_count, CAP).transpose(1, 0, 2).reshape(group_count, EXPERTS * CAP)
    picked = jax.vmap(take_rows)(slot_grad, position)
    input_grad = lax.optimization_barrier(jnp.sum(picked.astype(jnp.float32), axis=2)).astype(jnp.bfloat16).reshape(TOKENS, D)
    gate_grad = jax.vmap(take_rows)(slot_inner, position).reshape(TOKENS, 2)
    return (input_grad, gate_grad, first_grad, second_grad)
```

```python
import functools
import math

import jax
import jax.numpy as jnp
from jax import lax
from jax.experimental import pallas as pl
from jax.experimental.pallas import tpu as pltpu
from jax.sharding import PartitionSpec as P

coef_root = math.sqrt(2.0 / math.pi)


def gelu_pair(pre_value):
    cubic_term = 0.044715 * pre_value * pre_value * pre_value
    tanh_part = jnp.tanh(coef_root * (pre_value + cubic_term))
    activation = 0.5 * pre_value * (1.0 + tanh_part)
    derivative = 0.5 * (1.0 + tanh_part) + 0.5 * pre_value * (
        1.0 - tanh_part * tanh_part
    ) * coef_root * (1.0 + 3.0 * 0.044715 * pre_value * pre_value)
    return (activation, derivative)


def slot_tables(expert_ids, slot_ids, gate_values, experts, capacity):
    tok_count = expert_ids.shape[0]
    position = jnp.where(slot_ids >= 0, expert_ids * capacity + slot_ids, experts * capacity)
    flat_slots = position.reshape(-1)
    owners = jnp.repeat(jnp.arange(tok_count, dtype=jnp.int32), expert_ids.shape[1])
    owner_table = (
        jnp.full((experts * capacity,), tok_count, jnp.int32)
        .at[flat_slots]
        .set(owners, mode="drop")
    )
    gate_table = (
        jnp.zeros((experts * capacity,), gate_values.dtype)
        .at[flat_slots]
        .set(gate_values.reshape(-1), mode="drop")
    )
    return (position, owner_table, gate_table)


def build_slots(inputs, out_grad, expert_ids, slot_ids, gate_values, experts, capacity):
    position, owner_table, gate_table = slot_tables(
        expert_ids, slot_ids, gate_values, experts, capacity
    )
    feat_width = inputs.shape[1]
    dispatched = jnp.take(inputs, owner_table, axis=0, mode="fill", fill_value=0).reshape(
        experts, capacity, feat_width
    )
    cotangent = jnp.take(out_grad, owner_table, axis=0, mode="fill", fill_value=0).reshape(
        experts, capacity, feat_width
    )
    return (position, dispatched, cotangent, gate_table.reshape(experts, capacity))


def expert_work(slot_in, slot_cot, slot_gate, layer_in, layer_out):
    pre = jnp.dot(slot_in, layer_in, preferred_element_type=jnp.float32)
    act_full, derivative = gelu_pair(pre)
    activation = act_full.astype(jnp.bfloat16)
    back = lax.dot_general(
        slot_cot, layer_out, (((1,), (1,)), ((), ())), preferred_element_type=jnp.float32
    )
    inner_dot = jnp.sum(activation.astype(jnp.float32) * back, axis=1)
    gate_col = slot_gate.astype(jnp.float32)[:, None]
    scaled = (gate_col * slot_cot.astype(jnp.float32)).astype(jnp.bfloat16)
    hidden_grad = (gate_col * back * derivative).astype(jnp.bfloat16)
    in_grad = lax.dot_general(
        slot_in, hidden_grad, (((0,), (0,)), ((), ())), preferred_element_type=jnp.float32
    ).astype(jnp.bfloat16)
    out_grad_w = lax.dot_general(
        activation, scaled, (((0,), (0,)), ((), ())), preferred_element_type=jnp.float32
    ).astype(jnp.bfloat16)
    partial_value = lax.dot_general(
        hidden_grad, layer_in, (((1,), (1,)), ((), ())), preferred_element_type=jnp.float32
    )
    return (partial_value, inner_dot, in_grad, out_grad_w)


def per_device(inputs, out_grad, expert_ids, slot_ids, gate_values, first_layer, second_layer):
    experts = lax.axis_size("expert")
    tok_count = inputs.shape[0]
    feat_width = inputs.shape[1]
    capacity = expert_ids.shape[1] * tok_count // experts
    layer_in = first_layer[0]
    layer_out = second_layer[0]
    position, dispatched, cotangent, gate_slots = build_slots(
        inputs, out_grad, expert_ids, slot_ids, gate_values, experts, capacity
    )
    dispatched, cotangent, gate_slots = (
        lax.all_to_all(dispatched, "expert", split_axis=0, concat_axis=0, tiled=True),
        lax.all_to_all(cotangent, "expert", split_axis=0, concat_axis=0, tiled=True),
        lax.all_to_all(gate_slots, "expert", split_axis=0, concat_axis=0, tiled=True),
    )
    dispatched, cotangent, gate_slots = (
        lax.all_gather(dispatched.reshape(-1, feat_width), "dp", axis=0, tiled=True),
        lax.all_gather(cotangent.reshape(-1, feat_width), "dp", axis=0, tiled=True),
        lax.all_gather(gate_slots.reshape(-1), "dp", axis=0, tiled=True),
    )
    partial_value, inner_dot, first_grad, second_grad = expert_work(
        dispatched, cotangent, gate_slots, layer_in, layer_out
    )
    summed, inner_sum = (
        lax.psum_scatter(partial_value, "dp", scatter_dimension=0, tiled=True),
        lax.psum_scatter(inner_dot, "dp", scatter_dimension=0, tiled=True),
    )
    slot_grad = summed.astype(jnp.bfloat16).reshape(experts, capacity, feat_width)
    slot_inner = inner_sum.astype(jnp.bfloat16).reshape(experts, capacity)
    slot_grad, slot_inner = (
        lax.all_to_all(slot_grad, "expert", split_axis=0, concat_axis=0, tiled=True),
        lax.all_to_all(slot_inner, "expert", split_axis=0, concat_axis=0, tiled=True),
    )
    slot_grad = slot_grad.reshape(experts * capacity, feat_width)
    slot_inner = slot_inner.reshape(experts * capacity)
    picked = jnp.take(slot_grad, position, axis=0, mode="fill", fill_value=0)
    input_grad = jnp.sum(picked.astype(jnp.float32), axis=1).astype(jnp.bfloat16)
    gate_grad = jnp.take(slot_inner, position, axis=0, mode="fill", fill_value=0)
    return (input_grad, gate_grad, first_grad[None], second_grad[None])


SEND, ACROSS, BESIDE, PASS_ON, ADD_BESIDE, ADD_ACROSS, RETURN = range(7)


def fused_kernel(
    experts, capacity,
    in_ref, cot_ref, ids_ref, slots_ref, gate_ref, w1_hbm, w2_hbm,
    dx_ref, dgate_ref, dw1_hbm, dw2_hbm,
    w1, w2, pick, packed, slots, act, hidden, scaled, inner, part,
    got_beside, to_across, got_across, to_return, got_return, dw1, dw2,
    send_sem, recv_sem, load_sem, store_sem,
):
    f32, bf16 = jnp.float32, jnp.bfloat16
    width = in_ref.shape[1]
    hid = w1.shape[1]
    tile = 256
    pad = 128
    expert, dp = lax.axis_index("expert"), lax.axis_index("dp")
    core, half = dp % 2, dp // 2
    beside = dp + 1 - 2 * core
    across = (dp + 2) % 4
    mine = core * 2 + half
    from_across = core * 2 + 1 - half
    rows = 4 * capacity

    def peer(d):
        total, bit = 0, 1
        while bit < experts:
            total = total + ((expert // bit) % 2 + (d // bit) % 2) % 2 * bit
            bit *= 2
        return total

    def at(start, count, step):
        return pl.ds(pl.multiple_of(start, step), count)

    def block(ref, d, q):
        return ref.at[at(d * rows + q * capacity, capacity, capacity)]

    def remote(kind, d):
        if kind == SEND:
            src, dst = packed.at[at(d * capacity, capacity, capacity)], block(slots, d, mine)
            target = (peer(d), dp)
        elif kind in (ACROSS, BESIDE):
            src = dst = block(slots, d, mine)
            target = (expert, across if kind == ACROSS else beside)
        elif kind == PASS_ON:
            src = dst = block(slots, d, from_across)
            target = (expert, beside)
        elif kind == ADD_BESIDE:
            src = part.at[at(d * rows + (1 - core) * 2 * capacity, 2 * capacity, capacity)]
            dst = got_beside.at[at(d * 2 * capacity, 2 * capacity, capacity)]
            target = (expert, beside)
        elif kind == ADD_ACROSS:
            src = to_across.at[at(d * capacity, capacity, capacity)]
            dst = got_across.at[at(d * capacity, capacity, capacity)]
            target = (expert, across)
        else:
            src = to_return.at[at(d * capacity, capacity, capacity)]
            dst = got_return.at[at(d * capacity, capacity, capacity)]
            target = (peer(d), dp)
        return pltpu.make_async_remote_copy(
            src_ref=src, dst_ref=dst,
            send_sem=send_sem.at[kind, d], recv_sem=recv_sem.at[kind, d],
            device_id=target, device_id_type=pl.DeviceIdType.MESH,
        )

    barrier = pltpu.get_barrier_semaphore()
    for d in range(1, experts):
        pl.semaphore_signal(barrier, inc=1, device_id=(peer(d), dp), device_id_type=pl.DeviceIdType.MESH)
    for other in (across, beside):
        pl.semaphore_signal(barrier, inc=1, device_id=(expert, other), device_id_type=pl.DeviceIdType.MESH)
    load1 = pltpu.make_async_copy(w1_hbm.at[0], w1, load_sem.at[0])
    load2 = pltpu.make_async_copy(w2_hbm.at[0], w2, load_sem.at[1])
    load1.start()
    load2.start()

    total = experts * capacity
    column = lax.broadcasted_iota(jnp.int32, (in_ref.shape[0], total), 1)
    masks = []
    for k in range(2):
        slot = slots_ref[:, k : k + 1]
        place = jnp.where(slot >= 0, ids_ref[:, k : k + 1] * capacity + slot, total)
        masks.append((place ^ (expert * capacity)) == column)
    ones = [jnp.where(m, 1.0, 0.0).astype(f32) for m in masks]
    pick[0] = ones[0].astype(bf16)
    pick[1] = ones[1].astype(bf16)
    both = (ones[0] + ones[1]).astype(bf16)
    gates = (
        ones[0] * gate_ref[:, 0:1].astype(f32) + ones[1] * gate_ref[:, 1:2].astype(f32)
    ).astype(bf16)
    along = (((0,), (0,)), ((), ()))
    packed[:, 0:width] = lax.dot_general(both, in_ref[...], along, preferred_element_type=f32).astype(bf16)
    packed[:, width : 2 * width] = lax.dot_general(both, cot_ref[...], along, preferred_element_type=f32).astype(bf16)
    packed[:, 2 * width :] = lax.dot_general(
        gates, jnp.ones((in_ref.shape[0], pad), bf16), along, preferred_element_type=f32
    ).astype(bf16)
    slots[at(mine * capacity, capacity, capacity)] = packed[0:capacity]

    pl.semaphore_wait(barrier, experts + 1)
    remote(ACROSS, 0).start()
    remote(BESIDE, 0).start()
    for d in range(experts - 1, 0, -1):
        remote(SEND, d).start()

    pairs = experts // 2

    def forward(p):
        for d in (2 * p, 2 * p + 1):
            if d > 0:
                remote(SEND, d).wait_recv()
                remote(ACROSS, d).start()
                remote(BESIDE, d).start()

    def pass_on(p):
        for d in (2 * p, 2 * p + 1):
            remote(ACROSS, d).wait_recv()
            remote(PASS_ON, d).start()

    def compute(p):
        for d in (2 * p, 2 * p + 1):
            remote(BESIDE, d).wait_recv()
            remote(PASS_ON, d).wait_recv()
        span = slice(2 * p * rows, (2 * p + 2) * rows)
        inner[...] = jnp.zeros_like(inner)

        @pl.loop(0, hid // tile)
        def _(n):
            cols = at(n * tile, tile, tile)
            pre = jnp.dot(slots[span, 0:width], w1[:, cols], preferred_element_type=f32)
            back = lax.dot_general(
                slots[span, width : 2 * width], w2[cols, :], (((1,), (1,)), ((), ())),
                preferred_element_type=f32,
            )
            activation, derivative = gelu_pair(pre)
            activation = activation.astype(bf16)
            gate = slots[span, 2 * width :].astype(f32)[:, 0:1]
            act[span, cols] = activation
            hidden[span, cols] = (gate * back * derivative).astype(bf16)
            product = activation.astype(f32) * back
            inner[...] += product[:, 0:pad] + product[:, pad:]

        gate = slots[span, 2 * width :].astype(f32)[:, 0:1]
        scaled[span, :] = (gate * slots[span, width : 2 * width].astype(f32)).astype(bf16)

        @pl.loop(0, width // tile)
        def _(n):
            cols = at(n * tile, tile, tile)
            part[span, cols] = lax.dot_general(
                hidden[span, :], w1[cols, :], (((1,), (1,)), ((), ())), preferred_element_type=f32
            ).astype(bf16)

        part[span, width:] = jnp.broadcast_to(
            jnp.sum(inner[...], axis=1, keepdims=True), inner.shape
        ).astype(bf16)
        for d in (2 * p, 2 * p + 1):
            remote(ADD_BESIDE, d).start()

    def chip_sum(d, x):
        return (
            part[at(d * rows + (core * 2 + x) * capacity, capacity, capacity)].astype(f32)
            + got_beside[at(d * 2 * capacity + x * capacity, capacity, capacity)].astype(f32)
        )

    def add_across(p):
        for d in (2 * p, 2 * p + 1):
            remote(ADD_BESIDE, d).wait_recv()
            to_across[d * capacity : (d + 1) * capacity] = chip_sum(d, 1 - half).astype(bf16)
            remote(ADD_ACROSS, d).start()

    def give_back(p):
        for d in (2 * p, 2 * p + 1):
            span = slice(d * capacity, (d + 1) * capacity)
            remote(ADD_ACROSS, d).wait_recv()
            whole = (chip_sum(d, half) + got_across[span].astype(f32)).astype(bf16)
            if d == 0:
                got_return[span] = whole
            else:
                to_return[span] = whole
                remote(RETURN, d).start()

    def weight_tile(which, n):
        cols = at(n * tile, tile, tile)
        if which == 0:
            dw1[cols, :] = lax.dot_general(
                slots[:, cols], hidden[...], along, preferred_element_type=f32
            ).astype(bf16)
        else:
            dw2[cols, :] = lax.dot_general(
                act[:, cols], scaled[...], along, preferred_element_type=f32
            ).astype(bf16)

    def weight_grad(which):
        @pl.loop(0, (width if which == 0 else hid) // tile)
        def _(n):
            weight_tile(which, n)

        store = pltpu.make_async_copy(
            (dw1, dw2)[which], (dw1_hbm, dw2_hbm)[which].at[0], store_sem.at[which]
        )
        store.start()
        return store

    forward(0)
    load1.wait()
    load2.wait()
    if pairs > 1:
        forward(1)
    pass_on(0)
    for p in range(pairs):
        compute(p)
        if p + 2 < pairs:
            forward(p + 2)
        if p + 1 < pairs:
            pass_on(p + 1)
        if p >= 1:
            add_across(p - 1)
        if p >= 2:
            give_back(p - 2)
    add_across(pairs - 1)
    if pairs > 1:
        give_back(pairs - 2)
    store1 = weight_grad(0)
    give_back(pairs - 1)
    store2 = weight_grad(1)

    for d in range(1, experts):
        remote(RETURN, d).wait_recv()
    both = pick[0] + pick[1]
    dx_ref[...] = jnp.dot(both, got_return[:, 0:width], preferred_element_type=f32).astype(bf16)
    sides = [
        jnp.dot(pick[k], got_return[:, width:], preferred_element_type=f32)[:, 0:2] for k in range(2)
    ]
    lane = lax.broadcasted_iota(jnp.int32, sides[0].shape, 1)
    dgate_ref[...] = jnp.where(lane == 0, sides[0], sides[1]).astype(bf16)

    for d in range(experts):
        for kind in range(7):
            if d > 0 or kind not in (SEND, RETURN):
                remote(kind, d).wait_send()
    store1.wait()
    store2.wait()


def fused(inputs, out_grad, expert_ids, slot_ids, gate_values, first_layer, second_layer):
    experts = lax.axis_size("expert")
    tokens, width = inputs.shape
    capacity = expert_ids.shape[1] * tokens // experts
    hid = first_layer.shape[2]
    total = experts * capacity
    bf16, f32 = jnp.bfloat16, jnp.float32
    vmem = pl.BlockSpec(memory_space=pltpu.VMEM)
    hbm = pl.BlockSpec(memory_space=pl.ANY)
    flops = 10 * 4 * total * width * hid
    return pl.pallas_call(
        functools.partial(fused_kernel, experts, capacity),
        out_shape=(
            jax.ShapeDtypeStruct(inputs.shape, bf16),
            jax.ShapeDtypeStruct(gate_values.shape, bf16),
            jax.ShapeDtypeStruct(first_layer.shape, bf16),
            jax.ShapeDtypeStruct(second_layer.shape, bf16),
        ),
        in_specs=[vmem] * 5 + [hbm] * 2,
        out_specs=(vmem, vmem, hbm, hbm),
        scratch_shapes=[
            pltpu.VMEM((width, hid), bf16),
            pltpu.VMEM((hid, width), bf16),
            pltpu.VMEM((2, tokens, total), bf16),
            pltpu.VMEM((total, 2 * width + 128), bf16),
            pltpu.VMEM((4 * total, 2 * width + 128), bf16),
            pltpu.VMEM((4 * total, hid), bf16),
            pltpu.VMEM((4 * total, hid), bf16),
            pltpu.VMEM((4 * total, width), bf16),
            pltpu.VMEM((8 * capacity, 128), f32),
            pltpu.VMEM((4 * total, width + 128), bf16),
            pltpu.VMEM((2 * total, width + 128), bf16),
            pltpu.VMEM((total, width + 128), bf16),
            pltpu.VMEM((total, width + 128), bf16),
            pltpu.VMEM((total, width + 128), bf16),
            pltpu.VMEM((total, width + 128), bf16),
            pltpu.VMEM((width, hid), bf16),
            pltpu.VMEM((hid, width), bf16),
            pltpu.SemaphoreType.DMA((7, experts)),
            pltpu.SemaphoreType.DMA((7, experts)),
            pltpu.SemaphoreType.DMA((2,)),
            pltpu.SemaphoreType.DMA((2,)),
        ],
        compiler_params=pltpu.CompilerParams(
            collective_id=0, has_side_effects=True, vmem_limit_bytes=56 * 1024 * 1024
        ),
        cost_estimate=pl.CostEstimate(flops=flops, bytes_accessed=16 * width * hid, transcendentals=4 * total * hid),
    )(inputs, out_grad, expert_ids, slot_ids, gate_values, first_layer, second_layer)


def solution(mesh):
    placed = (
        P(("expert", "dp"), None),
        P(("expert", "dp"), None),
        P(("expert", "dp"), None),
        P(("expert", "dp"), None),
        P(("expert", "dp"), None),
        P("expert", None, "dp"),
        P("expert", "dp", None),
    )
    experts = mesh.shape["expert"]

    def chosen(inputs, out_grad, expert_ids, *rest):
        capacity = expert_ids.shape[1] * inputs.shape[0] // experts
        fits = capacity % 16 == 0 and experts & (experts - 1) == 0 and experts > 1
        fits = fits and mesh.shape["dp"] == 4 and capacity & (capacity - 1) == 0
        return (fused if fits else per_device)(inputs, out_grad, expert_ids, *rest)

    return jax.shard_map(
        chosen,
        mesh=mesh,
        in_specs=placed,
        out_specs=(
            P(("expert", "dp"), None),
            P(("expert", "dp"), None),
            P("expert", None, "dp"),
            P("expert", "dp", None),
        ),
        check_vma=False,
    )
```

```python
import functools
import math

import jax
import jax.numpy as jnp
from jax import lax
from jax.experimental import pallas as pl
from jax.experimental.pallas import tpu as pltpu
from jax.sharding import PartitionSpec as P

coef_root = math.sqrt(2.0 / math.pi)


def gelu_pair(pre_value):
    cubic_term = 0.044715 * pre_value * pre_value * pre_value
    tanh_part = jnp.tanh(coef_root * (pre_value + cubic_term))
    activation = 0.5 * pre_value * (1.0 + tanh_part)
    derivative = 0.5 * (1.0 + tanh_part) + 0.5 * pre_value * (
        1.0 - tanh_part * tanh_part
    ) * coef_root * (1.0 + 3.0 * 0.044715 * pre_value * pre_value)
    return (activation, derivative)


def slot_tables(expert_ids, slot_ids, gate_values, experts, capacity):
    tok_count = expert_ids.shape[0]
    position = jnp.where(slot_ids >= 0, expert_ids * capacity + slot_ids, experts * capacity)
    flat_slots = position.reshape(-1)
    owners = jnp.repeat(jnp.arange(tok_count, dtype=jnp.int32), expert_ids.shape[1])
    owner_table = (
        jnp.full((experts * capacity,), tok_count, jnp.int32)
        .at[flat_slots]
        .set(owners, mode="drop")
    )
    gate_table = (
        jnp.zeros((experts * capacity,), gate_values.dtype)
        .at[flat_slots]
        .set(gate_values.reshape(-1), mode="drop")
    )
    return (position, owner_table, gate_table)


def build_slots(inputs, out_grad, expert_ids, slot_ids, gate_values, experts, capacity):
    position, owner_table, gate_table = slot_tables(
        expert_ids, slot_ids, gate_values, experts, capacity
    )
    feat_width = inputs.shape[1]
    dispatched = jnp.take(inputs, owner_table, axis=0, mode="fill", fill_value=0).reshape(
        experts, capacity, feat_width
    )
    cotangent = jnp.take(out_grad, owner_table, axis=0, mode="fill", fill_value=0).reshape(
        experts, capacity, feat_width
    )
    return (position, dispatched, cotangent, gate_table.reshape(experts, capacity))


def expert_work(slot_in, slot_cot, slot_gate, layer_in, layer_out):
    pre = jnp.dot(slot_in, layer_in, preferred_element_type=jnp.float32)
    act_full, derivative = gelu_pair(pre)
    activation = act_full.astype(jnp.bfloat16)
    back = lax.dot_general(
        slot_cot, layer_out, (((1,), (1,)), ((), ())), preferred_element_type=jnp.float32
    )
    inner_dot = jnp.sum(activation.astype(jnp.float32) * back, axis=1)
    gate_col = slot_gate.astype(jnp.float32)[:, None]
    scaled = (gate_col * slot_cot.astype(jnp.float32)).astype(jnp.bfloat16)
    hidden_grad = (gate_col * back * derivative).astype(jnp.bfloat16)
    in_grad = lax.dot_general(
        slot_in, hidden_grad, (((0,), (0,)), ((), ())), preferred_element_type=jnp.float32
    ).astype(jnp.bfloat16)
    out_grad_w = lax.dot_general(
        activation, scaled, (((0,), (0,)), ((), ())), preferred_element_type=jnp.float32
    ).astype(jnp.bfloat16)
    partial_value = lax.dot_general(
        hidden_grad, layer_in, (((1,), (1,)), ((), ())), preferred_element_type=jnp.float32
    )
    return (partial_value, inner_dot, in_grad, out_grad_w)


def per_device(inputs, out_grad, expert_ids, slot_ids, gate_values, first_layer, second_layer):
    experts = lax.axis_size("expert")
    tok_count = inputs.shape[0]
    feat_width = inputs.shape[1]
    capacity = expert_ids.shape[1] * tok_count // experts
    layer_in = first_layer[0]
    layer_out = second_layer[0]
    position, dispatched, cotangent, gate_slots = build_slots(
        inputs, out_grad, expert_ids, slot_ids, gate_values, experts, capacity
    )
    dispatched, cotangent, gate_slots = (
        lax.all_to_all(dispatched, "expert", split_axis=0, concat_axis=0, tiled=True),
        lax.all_to_all(cotangent, "expert", split_axis=0, concat_axis=0, tiled=True),
        lax.all_to_all(gate_slots, "expert", split_axis=0, concat_axis=0, tiled=True),
    )
    dispatched, cotangent, gate_slots = (
        lax.all_gather(dispatched.reshape(-1, feat_width), "dp", axis=0, tiled=True),
        lax.all_gather(cotangent.reshape(-1, feat_width), "dp", axis=0, tiled=True),
        lax.all_gather(gate_slots.reshape(-1), "dp", axis=0, tiled=True),
    )
    partial_value, inner_dot, first_grad, second_grad = expert_work(
        dispatched, cotangent, gate_slots, layer_in, layer_out
    )
    summed, inner_sum = (
        lax.psum_scatter(partial_value, "dp", scatter_dimension=0, tiled=True),
        lax.psum_scatter(inner_dot, "dp", scatter_dimension=0, tiled=True),
    )
    slot_grad = summed.astype(jnp.bfloat16).reshape(experts, capacity, feat_width)
    slot_inner = inner_sum.astype(jnp.bfloat16).reshape(experts, capacity)
    slot_grad, slot_inner = (
        lax.all_to_all(slot_grad, "expert", split_axis=0, concat_axis=0, tiled=True),
        lax.all_to_all(slot_inner, "expert", split_axis=0, concat_axis=0, tiled=True),
    )
    slot_grad = slot_grad.reshape(experts * capacity, feat_width)
    slot_inner = slot_inner.reshape(experts * capacity)
    picked = jnp.take(slot_grad, position, axis=0, mode="fill", fill_value=0)
    input_grad = jnp.sum(picked.astype(jnp.float32), axis=1).astype(jnp.bfloat16)
    gate_grad = jnp.take(slot_inner, position, axis=0, mode="fill", fill_value=0)
    return (input_grad, gate_grad, first_grad[None], second_grad[None])


SEND, ACROSS, BESIDE, PASS_ON, ADD_BESIDE, ADD_ACROSS, RETURN = range(7)


def exchange_order(experts):
    half = experts // 2
    first = list(range(min(2, half)))
    order = list(first)
    for i in range(half):
        order.append(half + i)
        if len(first) + i < half:
            order.append(len(first) + i)
    return order


def fused_kernel(
    experts, capacity,
    in_ref, cot_ref, ids_ref, slots_ref, gate_ref, w1_hbm, w2_hbm,
    dx_ref, dgate_ref, dw1_hbm, dw2_hbm,
    w1, w2, pick, packed, slots, act, hidden, scaled, inner, part,
    got_beside, to_across, got_across, to_return, got_return, dw1, dw2,
    send_sem, recv_sem, load_sem, store_sem,
):
    f32, bf16 = jnp.float32, jnp.bfloat16
    width = in_ref.shape[1]
    hid = w1.shape[1]
    tile = 256
    pad = 128
    expert, dp = lax.axis_index("expert"), lax.axis_index("dp")
    core, half = dp % 2, dp // 2
    beside = dp + 1 - 2 * core
    across = (dp + 2) % 4
    mine = core * 2 + half
    from_across = core * 2 + 1 - half
    rows = 4 * capacity

    offsets = exchange_order(experts)

    def peer(d):
        d = offsets[d]
        total, bit = 0, 1
        while bit < experts:
            total = total + ((expert // bit) % 2 + (d // bit) % 2) % 2 * bit
            bit *= 2
        return total

    def at(start, count, step):
        return pl.ds(pl.multiple_of(start, step), count)

    def block(ref, d, q):
        return ref.at[at(d * rows + q * capacity, capacity, capacity)]

    def remote(kind, d):
        if kind == SEND:
            src = packed.at[at(offsets[d] * capacity, capacity, capacity)]
            dst = block(slots, d, mine)
            target = (peer(d), dp)
        elif kind in (ACROSS, BESIDE):
            src = dst = block(slots, d, mine)
            target = (expert, across if kind == ACROSS else beside)
        elif kind == PASS_ON:
            src = dst = block(slots, d, from_across)
            target = (expert, beside)
        elif kind == ADD_BESIDE:
            src = part.at[at(d * rows + (1 - core) * 2 * capacity, 2 * capacity, capacity)]
            dst = got_beside.at[at(d * 2 * capacity, 2 * capacity, capacity)]
            target = (expert, beside)
        elif kind == ADD_ACROSS:
            src = to_across.at[at(d * capacity, capacity, capacity)]
            dst = got_across.at[at(d * capacity, capacity, capacity)]
            target = (expert, across)
        else:
            src = to_return.at[at(d * capacity, capacity, capacity)]
            dst = got_return.at[at(offsets[d] * capacity, capacity, capacity)]
            target = (peer(d), dp)
        return pltpu.make_async_remote_copy(
            src_ref=src, dst_ref=dst,
            send_sem=send_sem.at[kind, d], recv_sem=recv_sem.at[kind, d],
            device_id=target, device_id_type=pl.DeviceIdType.MESH,
        )

    barrier = pltpu.get_barrier_semaphore()
    for d in range(1, experts):
        pl.semaphore_signal(barrier, inc=1, device_id=(peer(d), dp), device_id_type=pl.DeviceIdType.MESH)
    for other in (across, beside):
        pl.semaphore_signal(barrier, inc=1, device_id=(expert, other), device_id_type=pl.DeviceIdType.MESH)
    load1 = pltpu.make_async_copy(w1_hbm.at[0], w1, load_sem.at[0])
    load2 = pltpu.make_async_copy(w2_hbm.at[0], w2, load_sem.at[1])
    load1.start()
    load2.start()

    total = experts * capacity
    row = lax.broadcasted_iota(jnp.int32, (total, in_ref.shape[0]), 0)
    gate = gate_ref[...].astype(f32)
    ones = []
    for k in range(2):
        slot = slots_ref[k : k + 1, :]
        place = jnp.where(slot >= 0, ids_ref[k : k + 1, :] * capacity + slot, total)
        ones.append(jnp.where((place ^ (expert * capacity)) == row, 1.0, 0.0).astype(f32))
    pick[0] = ones[0].astype(bf16)
    pick[1] = ones[1].astype(bf16)
    both = (ones[0] + ones[1]).astype(bf16)
    gates = (ones[0] * gate[0:1, :] + ones[1] * gate[1:2, :]).astype(bf16)
    along = (((0,), (0,)), ((), ()))
    packed[:, 0:width] = jnp.dot(both, in_ref[...], preferred_element_type=f32).astype(bf16)
    packed[:, width : 2 * width] = jnp.dot(both, cot_ref[...], preferred_element_type=f32).astype(bf16)
    packed[:, 2 * width :] = jnp.dot(
        gates, jnp.ones((in_ref.shape[0], pad), bf16), preferred_element_type=f32
    ).astype(bf16)
    slots[at(mine * capacity, capacity, capacity)] = packed[0:capacity]

    pl.semaphore_wait(barrier, experts + 1)
    remote(ACROSS, 0).start()
    remote(BESIDE, 0).start()
    for d in range(1, experts):
        remote(SEND, d).start()

    pairs = experts // 2

    def forward(p):
        for d in (2 * p, 2 * p + 1):
            if d > 0:
                remote(SEND, d).wait_recv()
                remote(ACROSS, d).start()
                remote(BESIDE, d).start()

    def pass_on(p):
        for d in (2 * p, 2 * p + 1):
            remote(ACROSS, d).wait_recv()
            remote(PASS_ON, d).start()

    def compute(p):
        for d in (2 * p, 2 * p + 1):
            remote(BESIDE, d).wait_recv()
            remote(PASS_ON, d).wait_recv()
        span = slice(2 * p * rows, (2 * p + 2) * rows)
        inner[...] = jnp.zeros_like(inner)

        @pl.loop(0, hid // tile)
        def _(n):
            cols = at(n * tile, tile, tile)
            pre = jnp.dot(slots[span, 0:width], w1[:, cols], preferred_element_type=f32)
            back = lax.dot_general(
                slots[span, width : 2 * width], w2[cols, :], (((1,), (1,)), ((), ())),
                preferred_element_type=f32,
            )
            activation, derivative = gelu_pair(pre)
            activation = activation.astype(bf16)
            gate = slots[span, 2 * width :].astype(f32)[:, 0:1]
            act[span, cols] = activation
            hidden[span, cols] = (gate * back * derivative).astype(bf16)
            product = activation.astype(f32) * back
            inner[...] += product[:, 0:pad] + product[:, pad:]

        gate = slots[span, 2 * width :].astype(f32)[:, 0:1]
        scaled[span, :] = (gate * slots[span, width : 2 * width].astype(f32)).astype(bf16)

        @pl.loop(0, width // tile)
        def _(n):
            cols = at(n * tile, tile, tile)
            part[span, cols] = lax.dot_general(
                hidden[span, :], w1[cols, :], (((1,), (1,)), ((), ())), preferred_element_type=f32
            ).astype(bf16)

        part[span, width:] = jnp.broadcast_to(
            jnp.sum(inner[...], axis=1, keepdims=True), inner.shape
        ).astype(bf16)
        for d in (2 * p, 2 * p + 1):
            remote(ADD_BESIDE, d).start()

    def chip_sum(d, x):
        return (
            part[at(d * rows + (core * 2 + x) * capacity, capacity, capacity)].astype(f32)
            + got_beside[at(d * 2 * capacity + x * capacity, capacity, capacity)].astype(f32)
        )

    def add_across(p):
        for d in (2 * p, 2 * p + 1):
            remote(ADD_BESIDE, d).wait_recv()
            to_across[d * capacity : (d + 1) * capacity] = chip_sum(d, 1 - half).astype(bf16)
            remote(ADD_ACROSS, d).start()

    def give_back(p):
        for d in (2 * p, 2 * p + 1):
            span = slice(d * capacity, (d + 1) * capacity)
            remote(ADD_ACROSS, d).wait_recv()
            whole = (chip_sum(d, half) + got_across[span].astype(f32)).astype(bf16)
            if d == 0:
                got_return[span] = whole
            else:
                to_return[span] = whole
                remote(RETURN, d).start()

    def weight_tile(which, n):
        cols = at(n * tile, tile, tile)
        if which == 0:
            dw1[cols, :] = lax.dot_general(
                slots[:, cols], hidden[...], along, preferred_element_type=f32
            ).astype(bf16)
        else:
            dw2[cols, :] = lax.dot_general(
                act[:, cols], scaled[...], along, preferred_element_type=f32
            ).astype(bf16)

    def weight_grad(which):
        @pl.loop(0, (width if which == 0 else hid) // tile)
        def _(n):
            weight_tile(which, n)

        store = pltpu.make_async_copy(
            (dw1, dw2)[which], (dw1_hbm, dw2_hbm)[which].at[0], store_sem.at[which]
        )
        store.start()
        return store

    forward(0)
    if pairs > 1:
        forward(1)
    pass_on(0)
    load1.wait()
    load2.wait()
    for p in range(pairs):
        compute(p)
        if p + 2 < pairs:
            forward(p + 2)
        if p + 1 < pairs:
            pass_on(p + 1)
        if p >= 1:
            add_across(p - 1)
        if p >= 2:
            give_back(p - 2)
    add_across(pairs - 1)
    if pairs > 1:
        give_back(pairs - 2)
    store1 = weight_grad(0)
    give_back(pairs - 1)
    store2 = weight_grad(1)

    for d in range(1, experts):
        remote(RETURN, d).wait_recv()
    both = pick[0] + pick[1]
    dx_ref[...] = lax.dot_general(
        both, got_return[:, 0:width], along, preferred_element_type=f32
    ).astype(bf16)
    sides = [
        lax.dot_general(got_return[:, width:], pick[k], along, preferred_element_type=f32)[0:2]
        for k in range(2)
    ]
    side = lax.broadcasted_iota(jnp.int32, sides[0].shape, 0)
    dgate_ref[...] = jnp.where(side == 0, sides[0], sides[1]).astype(bf16)

    for d in range(experts):
        for kind in range(7):
            if d > 0 or kind not in (SEND, RETURN):
                remote(kind, d).wait_send()
    store1.wait()
    store2.wait()


def fused(inputs, out_grad, expert_ids, slot_ids, gate_values, first_layer, second_layer):
    experts = lax.axis_size("expert")
    tokens, width = inputs.shape
    capacity = expert_ids.shape[1] * tokens // experts
    hid = first_layer.shape[2]
    total = experts * capacity
    bf16, f32 = jnp.bfloat16, jnp.float32
    vmem = pl.BlockSpec(memory_space=pltpu.VMEM)
    hbm = pl.BlockSpec(memory_space=pl.ANY)
    flops = 10 * 4 * total * width * hid
    dx, dgate, dw1, dw2 = pl.pallas_call(
        functools.partial(fused_kernel, experts, capacity),
        out_shape=(
            jax.ShapeDtypeStruct(inputs.shape, bf16),
            jax.ShapeDtypeStruct(gate_values.shape[::-1], bf16),
            jax.ShapeDtypeStruct(first_layer.shape, bf16),
            jax.ShapeDtypeStruct(second_layer.shape, bf16),
        ),
        in_specs=[vmem] * 5 + [hbm] * 2,
        out_specs=(vmem, vmem, hbm, hbm),
        scratch_shapes=[
            pltpu.VMEM((width, hid), bf16),
            pltpu.VMEM((hid, width), bf16),
            pltpu.VMEM((2, total, tokens), bf16),
            pltpu.VMEM((total, 2 * width + 128), bf16),
            pltpu.VMEM((4 * total, 2 * width + 128), bf16),
            pltpu.VMEM((4 * total, hid), bf16),
            pltpu.VMEM((4 * total, hid), bf16),
            pltpu.VMEM((4 * total, width), bf16),
            pltpu.VMEM((8 * capacity, 128), f32),
            pltpu.VMEM((4 * total, width + 128), bf16),
            pltpu.VMEM((2 * total, width + 128), bf16),
            pltpu.VMEM((total, width + 128), bf16),
            pltpu.VMEM((total, width + 128), bf16),
            pltpu.VMEM((total, width + 128), bf16),
            pltpu.VMEM((total, width + 128), bf16),
            pltpu.VMEM((width, hid), bf16),
            pltpu.VMEM((hid, width), bf16),
            pltpu.SemaphoreType.DMA((7, experts)),
            pltpu.SemaphoreType.DMA((7, experts)),
            pltpu.SemaphoreType.DMA((2,)),
            pltpu.SemaphoreType.DMA((2,)),
        ],
        compiler_params=pltpu.CompilerParams(
            collective_id=0, has_side_effects=True, vmem_limit_bytes=56 * 1024 * 1024
        ),
        cost_estimate=pl.CostEstimate(flops=flops, bytes_accessed=16 * width * hid, transcendentals=4 * total * hid),
    )(inputs, out_grad, expert_ids.T, slot_ids.T, gate_values.T, first_layer, second_layer)
    return dx, dgate.T, dw1, dw2


def solution(mesh):
    placed = (
        P(("expert", "dp"), None),
        P(("expert", "dp"), None),
        P(("expert", "dp"), None),
        P(("expert", "dp"), None),
        P(("expert", "dp"), None),
        P("expert", None, "dp"),
        P("expert", "dp", None),
    )
    experts = mesh.shape["expert"]

    def chosen(inputs, out_grad, expert_ids, *rest):
        capacity = expert_ids.shape[1] * inputs.shape[0] // experts
        fits = capacity % 16 == 0 and experts & (experts - 1) == 0 and experts > 1
        fits = fits and mesh.shape["dp"] == 4 and capacity & (capacity - 1) == 0
        return (fused if fits else per_device)(inputs, out_grad, expert_ids, *rest)

    return jax.shard_map(
        chosen,
        mesh=mesh,
        in_specs=placed,
        out_specs=(
            P(("expert", "dp"), None),
            P(("expert", "dp"), None),
            P("expert", None, "dp"),
            P("expert", "dp", None),
        ),
        check_vma=False,
    )
```

```python
import functools
import math

import jax
import jax.numpy as jnp
from jax import lax
from jax.experimental import pallas as pl
from jax.experimental.pallas import tpu as pltpu
from jax.sharding import PartitionSpec as P

coef_root = math.sqrt(2.0 / math.pi)


def gelu_pair(pre_value):
    cubic_term = 0.044715 * pre_value * pre_value * pre_value
    tanh_part = jnp.tanh(coef_root * (pre_value + cubic_term))
    activation = 0.5 * pre_value * (1.0 + tanh_part)
    derivative = 0.5 * (1.0 + tanh_part) + 0.5 * pre_value * (
        1.0 - tanh_part * tanh_part
    ) * coef_root * (1.0 + 3.0 * 0.044715 * pre_value * pre_value)
    return (activation, derivative)


def slot_tables(expert_ids, slot_ids, gate_values, experts, capacity):
    tok_count = expert_ids.shape[0]
    position = jnp.where(slot_ids >= 0, expert_ids * capacity + slot_ids, experts * capacity)
    flat_slots = position.reshape(-1)
    owners = jnp.repeat(jnp.arange(tok_count, dtype=jnp.int32), expert_ids.shape[1])
    owner_table = (
        jnp.full((experts * capacity,), tok_count, jnp.int32)
        .at[flat_slots]
        .set(owners, mode="drop")
    )
    gate_table = (
        jnp.zeros((experts * capacity,), gate_values.dtype)
        .at[flat_slots]
        .set(gate_values.reshape(-1), mode="drop")
    )
    return (position, owner_table, gate_table)


def build_slots(inputs, out_grad, expert_ids, slot_ids, gate_values, experts, capacity):
    position, owner_table, gate_table = slot_tables(
        expert_ids, slot_ids, gate_values, experts, capacity
    )
    feat_width = inputs.shape[1]
    dispatched = jnp.take(inputs, owner_table, axis=0, mode="fill", fill_value=0).reshape(
        experts, capacity, feat_width
    )
    cotangent = jnp.take(out_grad, owner_table, axis=0, mode="fill", fill_value=0).reshape(
        experts, capacity, feat_width
    )
    return (position, dispatched, cotangent, gate_table.reshape(experts, capacity))


def expert_work(slot_in, slot_cot, slot_gate, layer_in, layer_out):
    pre = jnp.dot(slot_in, layer_in, preferred_element_type=jnp.float32)
    act_full, derivative = gelu_pair(pre)
    activation = act_full.astype(jnp.bfloat16)
    back = lax.dot_general(
        slot_cot, layer_out, (((1,), (1,)), ((), ())), preferred_element_type=jnp.float32
    )
    inner_dot = jnp.sum(activation.astype(jnp.float32) * back, axis=1)
    gate_col = slot_gate.astype(jnp.float32)[:, None]
    scaled = (gate_col * slot_cot.astype(jnp.float32)).astype(jnp.bfloat16)
    hidden_grad = (gate_col * back * derivative).astype(jnp.bfloat16)
    in_grad = lax.dot_general(
        slot_in, hidden_grad, (((0,), (0,)), ((), ())), preferred_element_type=jnp.float32
    ).astype(jnp.bfloat16)
    out_grad_w = lax.dot_general(
        activation, scaled, (((0,), (0,)), ((), ())), preferred_element_type=jnp.float32
    ).astype(jnp.bfloat16)
    partial_value = lax.dot_general(
        hidden_grad, layer_in, (((1,), (1,)), ((), ())), preferred_element_type=jnp.float32
    )
    return (partial_value, inner_dot, in_grad, out_grad_w)


def per_device(inputs, out_grad, expert_ids, slot_ids, gate_values, first_layer, second_layer):
    experts = lax.axis_size("expert")
    tok_count = inputs.shape[0]
    feat_width = inputs.shape[1]
    capacity = expert_ids.shape[1] * tok_count // experts
    layer_in = first_layer[0]
    layer_out = second_layer[0]
    position, dispatched, cotangent, gate_slots = build_slots(
        inputs, out_grad, expert_ids, slot_ids, gate_values, experts, capacity
    )
    dispatched, cotangent, gate_slots = (
        lax.all_to_all(dispatched, "expert", split_axis=0, concat_axis=0, tiled=True),
        lax.all_to_all(cotangent, "expert", split_axis=0, concat_axis=0, tiled=True),
        lax.all_to_all(gate_slots, "expert", split_axis=0, concat_axis=0, tiled=True),
    )
    dispatched, cotangent, gate_slots = (
        lax.all_gather(dispatched.reshape(-1, feat_width), "dp", axis=0, tiled=True),
        lax.all_gather(cotangent.reshape(-1, feat_width), "dp", axis=0, tiled=True),
        lax.all_gather(gate_slots.reshape(-1), "dp", axis=0, tiled=True),
    )
    partial_value, inner_dot, first_grad, second_grad = expert_work(
        dispatched, cotangent, gate_slots, layer_in, layer_out
    )
    summed, inner_sum = (
        lax.psum_scatter(partial_value, "dp", scatter_dimension=0, tiled=True),
        lax.psum_scatter(inner_dot, "dp", scatter_dimension=0, tiled=True),
    )
    slot_grad = summed.astype(jnp.bfloat16).reshape(experts, capacity, feat_width)
    slot_inner = inner_sum.astype(jnp.bfloat16).reshape(experts, capacity)
    slot_grad, slot_inner = (
        lax.all_to_all(slot_grad, "expert", split_axis=0, concat_axis=0, tiled=True),
        lax.all_to_all(slot_inner, "expert", split_axis=0, concat_axis=0, tiled=True),
    )
    slot_grad = slot_grad.reshape(experts * capacity, feat_width)
    slot_inner = slot_inner.reshape(experts * capacity)
    picked = jnp.take(slot_grad, position, axis=0, mode="fill", fill_value=0)
    input_grad = jnp.sum(picked.astype(jnp.float32), axis=1).astype(jnp.bfloat16)
    gate_grad = jnp.take(slot_inner, position, axis=0, mode="fill", fill_value=0)
    return (input_grad, gate_grad, first_grad[None], second_grad[None])


SEND, ACROSS, BESIDE, PASS_ON, ADD_BESIDE, ADD_ACROSS, RETURN = range(7)


def exchange_order(experts):
    half = experts // 2
    first = list(range(min(2, half)))
    order = list(first)
    for i in range(half):
        order.append(half + i)
        if len(first) + i < half:
            order.append(len(first) + i)
    return order


def fused_kernel(
    experts, capacity,
    in_ref, cot_ref, ids_ref, slots_ref, gate_ref, w1_hbm, w2_hbm,
    dx_ref, dgate_ref, dw1_hbm, dw2_hbm,
    w1, w2, pick, packed, slots, act, hidden, scaled, inner, part,
    got_beside, to_across, got_across, to_return, got_return, dw1, dw2,
    send_sem, recv_sem, load_sem, store_sem,
):
    f32, bf16 = jnp.float32, jnp.bfloat16
    width = in_ref.shape[1]
    hid = w1.shape[1]
    tile = 256
    pad = 128
    expert, dp = lax.axis_index("expert"), lax.axis_index("dp")
    core, half = dp % 2, dp // 2
    beside = dp + 1 - 2 * core
    across = (dp + 2) % 4
    mine = core * 2 + half
    from_across = core * 2 + 1 - half
    rows = 4 * capacity

    offsets = exchange_order(experts)

    def peer(d):
        d = offsets[d]
        total, bit = 0, 1
        while bit < experts:
            total = total + ((expert // bit) % 2 + (d // bit) % 2) % 2 * bit
            bit *= 2
        return total

    def at(start, count, step):
        return pl.ds(pl.multiple_of(start, step), count)

    def block(ref, d, q):
        return ref.at[at(d * rows + q * capacity, capacity, capacity)]

    def remote(kind, d):
        if kind == SEND:
            src = packed.at[at(offsets[d] * capacity, capacity, capacity)]
            dst = block(slots, d, mine)
            target = (peer(d), dp)
        elif kind in (ACROSS, BESIDE):
            src = dst = block(slots, d, mine)
            target = (expert, across if kind == ACROSS else beside)
        elif kind == PASS_ON:
            src = dst = block(slots, d, from_across)
            target = (expert, beside)
        elif kind == ADD_BESIDE:
            src = part.at[at(d * rows + (1 - core) * 2 * capacity, 2 * capacity, capacity)]
            dst = got_beside.at[at(d * 2 * capacity, 2 * capacity, capacity)]
            target = (expert, beside)
        elif kind == ADD_ACROSS:
            src = to_across.at[at(d * capacity, capacity, capacity)]
            dst = got_across.at[at(d * capacity, capacity, capacity)]
            target = (expert, across)
        else:
            src = to_return.at[at(d * capacity, capacity, capacity)]
            dst = got_return.at[at(offsets[d] * capacity, capacity, capacity)]
            target = (peer(d), dp)
        return pltpu.make_async_remote_copy(
            src_ref=src, dst_ref=dst,
            send_sem=send_sem.at[kind, d], recv_sem=recv_sem.at[kind, d],
            device_id=target, device_id_type=pl.DeviceIdType.MESH,
        )

    barrier = pltpu.get_barrier_semaphore()
    for d in range(1, experts):
        pl.semaphore_signal(barrier, inc=1, device_id=(peer(d), dp), device_id_type=pl.DeviceIdType.MESH)
    for other in (across, beside):
        pl.semaphore_signal(barrier, inc=1, device_id=(expert, other), device_id_type=pl.DeviceIdType.MESH)
    load1 = pltpu.make_async_copy(w1_hbm.at[0], w1, load_sem.at[0])
    load2 = pltpu.make_async_copy(w2_hbm.at[0], w2, load_sem.at[1])
    load1.start()
    load2.start()

    total = experts * capacity
    row = lax.broadcasted_iota(jnp.int32, (total, in_ref.shape[0]), 0)
    gate = gate_ref[...].astype(f32)
    ones = []
    for k in range(2):
        slot = slots_ref[k : k + 1, :]
        place = jnp.where(slot >= 0, ids_ref[k : k + 1, :] * capacity + slot, total)
        ones.append(jnp.where((place ^ (expert * capacity)) == row, 1.0, 0.0).astype(f32))
    pick[0] = ones[0].astype(bf16)
    pick[1] = ones[1].astype(bf16)
    both = (ones[0] + ones[1]).astype(bf16)
    gates = (ones[0] * gate[0:1, :] + ones[1] * gate[1:2, :]).astype(bf16)
    along = (((0,), (0,)), ((), ()))
    packed[:, 0:width] = jnp.dot(both, in_ref[...], preferred_element_type=f32).astype(bf16)
    packed[:, width : 2 * width] = jnp.dot(both, cot_ref[...], preferred_element_type=f32).astype(bf16)
    packed[:, 2 * width :] = jnp.dot(
        gates, jnp.ones((in_ref.shape[0], pad), bf16), preferred_element_type=f32
    ).astype(bf16)
    slots[at(mine * capacity, capacity, capacity)] = packed[0:capacity]

    pl.semaphore_wait(barrier, experts + 1)
    remote(ACROSS, 0).start()
    remote(BESIDE, 0).start()
    for d in range(1, experts):
        remote(SEND, d).start()

    pairs = experts // 2

    def forward(p):
        for d in (2 * p, 2 * p + 1):
            if d > 0:
                remote(SEND, d).wait_recv()
                remote(ACROSS, d).start()
                remote(BESIDE, d).start()

    def pass_on(p):
        for d in (2 * p, 2 * p + 1):
            remote(ACROSS, d).wait_recv()
            remote(PASS_ON, d).start()

    def compute(p):
        for d in (2 * p, 2 * p + 1):
            remote(BESIDE, d).wait_recv()
            remote(PASS_ON, d).wait_recv()
        span = slice(2 * p * rows, (2 * p + 2) * rows)
        inner[...] = jnp.zeros_like(inner)

        @pl.loop(0, hid // tile)
        def _(n):
            cols = at(n * tile, tile, tile)
            pre = jnp.dot(slots[span, 0:width], w1[:, cols], preferred_element_type=f32)
            back = lax.dot_general(
                slots[span, width : 2 * width], w2[cols, :], (((1,), (1,)), ((), ())),
                preferred_element_type=f32,
            )
            activation, derivative = gelu_pair(pre)
            activation = activation.astype(bf16)
            gate = slots[span, 2 * width :].astype(f32)[:, 0:1]
            act[span, cols] = activation
            hidden[span, cols] = (gate * back * derivative).astype(bf16)
            product = activation.astype(f32) * back
            inner[...] += product[:, 0:pad] + product[:, pad:]

        gate = slots[span, 2 * width :].astype(f32)[:, 0:1]
        scaled[span, :] = (gate * slots[span, width : 2 * width].astype(f32)).astype(bf16)

        @pl.loop(0, width // tile)
        def _(n):
            cols = at(n * tile, tile, tile)
            part[span, cols] = lax.dot_general(
                hidden[span, :], w1[cols, :], (((1,), (1,)), ((), ())), preferred_element_type=f32
            ).astype(bf16)

        part[span, width:] = jnp.broadcast_to(
            jnp.sum(inner[...], axis=1, keepdims=True), inner.shape
        ).astype(bf16)
        for d in (2 * p, 2 * p + 1):
            remote(ADD_BESIDE, d).start()

    def chip_sum(d, x):
        return (
            part[at(d * rows + (core * 2 + x) * capacity, capacity, capacity)].astype(f32)
            + got_beside[at(d * 2 * capacity + x * capacity, capacity, capacity)].astype(f32)
        )

    def add_across(p):
        for d in (2 * p, 2 * p + 1):
            remote(ADD_BESIDE, d).wait_recv()
            to_across[d * capacity : (d + 1) * capacity] = chip_sum(d, 1 - half).astype(bf16)
            remote(ADD_ACROSS, d).start()

    def give_back(p):
        for d in (2 * p, 2 * p + 1):
            span = slice(d * capacity, (d + 1) * capacity)
            remote(ADD_ACROSS, d).wait_recv()
            whole = (chip_sum(d, half) + got_across[span].astype(f32)).astype(bf16)
            if d == 0:
                got_return[span] = whole
            else:
                to_return[span] = whole
                remote(RETURN, d).start()

    def weight_tile(which, n):
        cols = at(n * tile, tile, tile)
        if which == 0:
            dw1[cols, :] = lax.dot_general(
                slots[:, cols], hidden[...], along, preferred_element_type=f32
            ).astype(bf16)
        else:
            dw2[cols, :] = lax.dot_general(
                act[:, cols], scaled[...], along, preferred_element_type=f32
            ).astype(bf16)

    def weight_grad(which):
        @pl.loop(0, (width if which == 0 else hid) // tile)
        def _(n):
            weight_tile(which, n)

        store = pltpu.make_async_copy(
            (dw1, dw2)[which], (dw1_hbm, dw2_hbm)[which].at[0], store_sem.at[which]
        )
        store.start()
        return store

    forward(0)
    if pairs > 1:
        forward(1)
    pass_on(0)
    load1.wait()
    load2.wait()
    for p in range(pairs):
        compute(p)
        if p + 2 < pairs:
            forward(p + 2)
        add_across(p)
        if p + 1 < pairs:
            pass_on(p + 1)
        if p >= 1:
            give_back(p - 1)
    store1 = weight_grad(0)
    give_back(pairs - 1)
    store2 = weight_grad(1)

    for d in range(1, experts):
        remote(RETURN, d).wait_recv()
    both = pick[0] + pick[1]
    dx_ref[...] = lax.dot_general(
        both, got_return[:, 0:width], along, preferred_element_type=f32
    ).astype(bf16)
    sides = [
        lax.dot_general(got_return[:, width:], pick[k], along, preferred_element_type=f32)[0:2]
        for k in range(2)
    ]
    side = lax.broadcasted_iota(jnp.int32, sides[0].shape, 0)
    dgate_ref[...] = jnp.where(side == 0, sides[0], sides[1]).astype(bf16)

    for d in range(experts):
        for kind in range(7):
            if d > 0 or kind not in (SEND, RETURN):
                remote(kind, d).wait_send()
    store1.wait()
    store2.wait()


def hand_over_kernel(pieces, *refs):
    count = len(pieces)
    sources, results, held = refs[:count], refs[count : 2 * count], refs[2 * count : 3 * count]
    load_sem, store_sem = refs[3 * count :]
    moves = []
    for i, split in enumerate(pieces):
        height = sources[i].shape[0] // split
        for j in range(split):
            part = pl.ds(j * height, height)
            n = len(moves)
            moves.append((
                pltpu.make_async_copy(sources[i].at[part], held[i].at[part], load_sem.at[n]),
                pltpu.make_async_copy(held[i].at[part], results[i].at[part], store_sem.at[n]),
            ))
    for load, _ in moves:
        load.start()
    for load, store in moves:
        load.wait()
        store.start()
    for _, store in moves:
        store.wait()


def hand_over(arrays, pieces):
    hbm = pl.BlockSpec(memory_space=pl.ANY)
    shapes = tuple(jax.ShapeDtypeStruct(a.shape, a.dtype) for a in arrays)
    return pl.pallas_call(
        functools.partial(hand_over_kernel, pieces),
        out_shape=shapes,
        in_specs=[hbm] * len(arrays),
        out_specs=(hbm,) * len(arrays),
        scratch_shapes=[pltpu.VMEM(a.shape, a.dtype) for a in arrays]
        + [pltpu.SemaphoreType.DMA((sum(pieces),))] * 2,
        compiler_params=pltpu.CompilerParams(vmem_limit_bytes=56 * 1024 * 1024),
    )(*arrays)


def fused(inputs, out_grad, expert_ids, slot_ids, gate_values, first_layer, second_layer):
    experts = lax.axis_size("expert")
    tokens, width = inputs.shape
    capacity = expert_ids.shape[1] * tokens // experts
    hid = first_layer.shape[2]
    total = experts * capacity
    bf16, f32 = jnp.bfloat16, jnp.float32
    vmem = pl.BlockSpec(memory_space=pltpu.VMEM)
    hbm = pl.BlockSpec(memory_space=pl.ANY)
    flops = 10 * 4 * total * width * hid
    dx, dgate, dw1, dw2 = pl.pallas_call(
        functools.partial(fused_kernel, experts, capacity),
        out_shape=(
            jax.ShapeDtypeStruct(inputs.shape, bf16),
            jax.ShapeDtypeStruct(gate_values.shape[::-1], bf16),
            jax.ShapeDtypeStruct(first_layer.shape, bf16),
            jax.ShapeDtypeStruct(second_layer.shape, bf16),
        ),
        in_specs=[vmem] * 5 + [hbm] * 2,
        out_specs=(vmem, vmem, hbm, hbm),
        scratch_shapes=[
            pltpu.VMEM((width, hid), bf16),
            pltpu.VMEM((hid, width), bf16),
            pltpu.VMEM((2, total, tokens), bf16),
            pltpu.VMEM((total, 2 * width + 128), bf16),
            pltpu.VMEM((4 * total, 2 * width + 128), bf16),
            pltpu.VMEM((4 * total, hid), bf16),
            pltpu.VMEM((4 * total, hid), bf16),
            pltpu.VMEM((4 * total, width), bf16),
            pltpu.VMEM((8 * capacity, 128), f32),
            pltpu.VMEM((4 * total, width + 128), bf16),
            pltpu.VMEM((2 * total, width + 128), bf16),
            pltpu.VMEM((total, width + 128), bf16),
            pltpu.VMEM((total, width + 128), bf16),
            pltpu.VMEM((total, width + 128), bf16),
            pltpu.VMEM((total, width + 128), bf16),
            pltpu.VMEM((width, hid), bf16),
            pltpu.VMEM((hid, width), bf16),
            pltpu.SemaphoreType.DMA((7, experts)),
            pltpu.SemaphoreType.DMA((7, experts)),
            pltpu.SemaphoreType.DMA((2,)),
            pltpu.SemaphoreType.DMA((2,)),
        ],
        compiler_params=pltpu.CompilerParams(
            collective_id=0, has_side_effects=True, vmem_limit_bytes=56 * 1024 * 1024
        ),
        cost_estimate=pl.CostEstimate(flops=flops, bytes_accessed=16 * width * hid, transcendentals=4 * total * hid),
    )(inputs, out_grad, expert_ids.T, slot_ids.T, gate_values.T, first_layer, second_layer)
    first_grad, second_grad, dx, dgate = hand_over((dw1[0], dw2[0], dx, dgate), (4, 4, 1, 1))
    return dx, dgate.T, first_grad[None], second_grad[None]


def solution(mesh):
    placed = (
        P(("expert", "dp"), None),
        P(("expert", "dp"), None),
        P(("expert", "dp"), None),
        P(("expert", "dp"), None),
        P(("expert", "dp"), None),
        P("expert", None, "dp"),
        P("expert", "dp", None),
    )
    experts = mesh.shape["expert"]

    def chosen(inputs, out_grad, expert_ids, *rest):
        capacity = expert_ids.shape[1] * inputs.shape[0] // experts
        fits = capacity % 16 == 0 and experts & (experts - 1) == 0 and experts > 1
        fits = fits and mesh.shape["dp"] == 4 and capacity & (capacity - 1) == 0
        return (fused if fits else per_device)(inputs, out_grad, expert_ids, *rest)

    return jax.shard_map(
        chosen,
        mesh=mesh,
        in_specs=placed,
        out_specs=(
            P(("expert", "dp"), None),
            P(("expert", "dp"), None),
            P("expert", None, "dp"),
            P("expert", "dp", None),
        ),
        check_vma=False,
    )
```

```python
import functools
import math

import jax
import jax.numpy as jnp
from jax import lax
from jax.experimental import pallas as pl
from jax.experimental.pallas import tpu as pltpu
from jax.sharding import PartitionSpec as P

coef_root = math.sqrt(2.0 / math.pi)


def gelu_pair(pre_value):
    cubic_term = 0.044715 * pre_value * pre_value * pre_value
    tanh_part = jnp.tanh(coef_root * (pre_value + cubic_term))
    activation = 0.5 * pre_value * (1.0 + tanh_part)
    derivative = 0.5 * (1.0 + tanh_part) + 0.5 * pre_value * (
        1.0 - tanh_part * tanh_part
    ) * coef_root * (1.0 + 3.0 * 0.044715 * pre_value * pre_value)
    return (activation, derivative)


def slot_tables(expert_ids, slot_ids, gate_values, experts, capacity):
    tok_count = expert_ids.shape[0]
    position = jnp.where(slot_ids >= 0, expert_ids * capacity + slot_ids, experts * capacity)
    flat_slots = position.reshape(-1)
    owners = jnp.repeat(jnp.arange(tok_count, dtype=jnp.int32), expert_ids.shape[1])
    owner_table = (
        jnp.full((experts * capacity,), tok_count, jnp.int32)
        .at[flat_slots]
        .set(owners, mode="drop")
    )
    gate_table = (
        jnp.zeros((experts * capacity,), gate_values.dtype)
        .at[flat_slots]
        .set(gate_values.reshape(-1), mode="drop")
    )
    return (position, owner_table, gate_table)


def build_slots(inputs, out_grad, expert_ids, slot_ids, gate_values, experts, capacity):
    position, owner_table, gate_table = slot_tables(
        expert_ids, slot_ids, gate_values, experts, capacity
    )
    feat_width = inputs.shape[1]
    dispatched = jnp.take(inputs, owner_table, axis=0, mode="fill", fill_value=0).reshape(
        experts, capacity, feat_width
    )
    cotangent = jnp.take(out_grad, owner_table, axis=0, mode="fill", fill_value=0).reshape(
        experts, capacity, feat_width
    )
    return (position, dispatched, cotangent, gate_table.reshape(experts, capacity))


def expert_work(slot_in, slot_cot, slot_gate, layer_in, layer_out):
    pre = jnp.dot(slot_in, layer_in, preferred_element_type=jnp.float32)
    act_full, derivative = gelu_pair(pre)
    activation = act_full.astype(jnp.bfloat16)
    back = lax.dot_general(
        slot_cot, layer_out, (((1,), (1,)), ((), ())), preferred_element_type=jnp.float32
    )
    inner_dot = jnp.sum(activation.astype(jnp.float32) * back, axis=1)
    gate_col = slot_gate.astype(jnp.float32)[:, None]
    scaled = (gate_col * slot_cot.astype(jnp.float32)).astype(jnp.bfloat16)
    hidden_grad = (gate_col * back * derivative).astype(jnp.bfloat16)
    in_grad = lax.dot_general(
        slot_in, hidden_grad, (((0,), (0,)), ((), ())), preferred_element_type=jnp.float32
    ).astype(jnp.bfloat16)
    out_grad_w = lax.dot_general(
        activation, scaled, (((0,), (0,)), ((), ())), preferred_element_type=jnp.float32
    ).astype(jnp.bfloat16)
    partial_value = lax.dot_general(
        hidden_grad, layer_in, (((1,), (1,)), ((), ())), preferred_element_type=jnp.float32
    )
    return (partial_value, inner_dot, in_grad, out_grad_w)


def per_device(inputs, out_grad, expert_ids, slot_ids, gate_values, first_layer, second_layer):
    experts = lax.axis_size("expert")
    tok_count = inputs.shape[0]
    feat_width = inputs.shape[1]
    capacity = expert_ids.shape[1] * tok_count // experts
    layer_in = first_layer[0]
    layer_out = second_layer[0]
    position, dispatched, cotangent, gate_slots = build_slots(
        inputs, out_grad, expert_ids, slot_ids, gate_values, experts, capacity
    )
    dispatched, cotangent, gate_slots = (
        lax.all_to_all(dispatched, "expert", split_axis=0, concat_axis=0, tiled=True),
        lax.all_to_all(cotangent, "expert", split_axis=0, concat_axis=0, tiled=True),
        lax.all_to_all(gate_slots, "expert", split_axis=0, concat_axis=0, tiled=True),
    )
    dispatched, cotangent, gate_slots = (
        lax.all_gather(dispatched.reshape(-1, feat_width), "dp", axis=0, tiled=True),
        lax.all_gather(cotangent.reshape(-1, feat_width), "dp", axis=0, tiled=True),
        lax.all_gather(gate_slots.reshape(-1), "dp", axis=0, tiled=True),
    )
    partial_value, inner_dot, first_grad, second_grad = expert_work(
        dispatched, cotangent, gate_slots, layer_in, layer_out
    )
    summed, inner_sum = (
        lax.psum_scatter(partial_value, "dp", scatter_dimension=0, tiled=True),
        lax.psum_scatter(inner_dot, "dp", scatter_dimension=0, tiled=True),
    )
    slot_grad = summed.astype(jnp.bfloat16).reshape(experts, capacity, feat_width)
    slot_inner = inner_sum.astype(jnp.bfloat16).reshape(experts, capacity)
    slot_grad, slot_inner = (
        lax.all_to_all(slot_grad, "expert", split_axis=0, concat_axis=0, tiled=True),
        lax.all_to_all(slot_inner, "expert", split_axis=0, concat_axis=0, tiled=True),
    )
    slot_grad = slot_grad.reshape(experts * capacity, feat_width)
    slot_inner = slot_inner.reshape(experts * capacity)
    picked = jnp.take(slot_grad, position, axis=0, mode="fill", fill_value=0)
    input_grad = jnp.sum(picked.astype(jnp.float32), axis=1).astype(jnp.bfloat16)
    gate_grad = jnp.take(slot_inner, position, axis=0, mode="fill", fill_value=0)
    return (input_grad, gate_grad, first_grad[None], second_grad[None])


SEND, ACROSS, BESIDE, PASS_ON, ADD_BESIDE, ADD_ACROSS, RETURN = range(7)


def exchange_order(experts):
    half = experts // 2
    first = list(range(min(2, half)))
    order = list(first)
    for i in range(half):
        order.append(half + i)
        if len(first) + i < half:
            order.append(len(first) + i)
    return order


def fused_kernel(
    experts, capacity,
    in_ref, cot_ref, ids_ref, slots_ref, gate_ref, w1_hbm, w2_hbm,
    dx_ref, dgate_ref, dw1_hbm, dw2_hbm,
    w1, w2, pick, packed, slots, act, hidden, scaled, inner, part,
    got_beside, to_across, got_across, to_return, got_return, dw1, dw2,
    send_sem, recv_sem, load_sem, store_sem,
):
    f32, bf16 = jnp.float32, jnp.bfloat16
    width = in_ref.shape[1]
    hid = w1.shape[1]
    tile = 512
    pad = 128
    expert, dp = lax.axis_index("expert"), lax.axis_index("dp")
    core, half = dp % 2, dp // 2
    beside = dp + 1 - 2 * core
    across = (dp + 2) % 4
    mine = core * 2 + half
    from_across = core * 2 + 1 - half
    rows = 4 * capacity

    offsets = exchange_order(experts)

    def peer(d):
        d = offsets[d]
        total, bit = 0, 1
        while bit < experts:
            total = total + ((expert // bit) % 2 + (d // bit) % 2) % 2 * bit
            bit *= 2
        return total

    def at(start, count, step):
        return pl.ds(pl.multiple_of(start, step), count)

    def block(ref, d, q):
        return ref.at[at(d * rows + q * capacity, capacity, capacity)]

    def remote(kind, d):
        if kind == SEND:
            src = packed.at[at(offsets[d] * capacity, capacity, capacity)]
            dst = block(slots, d, mine)
            target = (peer(d), dp)
        elif kind in (ACROSS, BESIDE):
            src = dst = block(slots, d, mine)
            target = (expert, across if kind == ACROSS else beside)
        elif kind == PASS_ON:
            src = dst = block(slots, d, from_across)
            target = (expert, beside)
        elif kind == ADD_BESIDE:
            src = part.at[at(d * rows + (1 - core) * 2 * capacity, 2 * capacity, capacity)]
            dst = got_beside.at[at(d * 2 * capacity, 2 * capacity, capacity)]
            target = (expert, beside)
        elif kind == ADD_ACROSS:
            src = to_across.at[at(d * capacity, capacity, capacity)]
            dst = got_across.at[at(d * capacity, capacity, capacity)]
            target = (expert, across)
        else:
            src = to_return.at[at(d * capacity, capacity, capacity)]
            dst = got_return.at[at(offsets[d] * capacity, capacity, capacity)]
            target = (peer(d), dp)
        return pltpu.make_async_remote_copy(
            src_ref=src, dst_ref=dst,
            send_sem=send_sem.at[kind, d], recv_sem=recv_sem.at[kind, d],
            device_id=target, device_id_type=pl.DeviceIdType.MESH,
        )

    barrier = pltpu.get_barrier_semaphore()
    for d in range(1, experts):
        pl.semaphore_signal(barrier, inc=1, device_id=(peer(d), dp), device_id_type=pl.DeviceIdType.MESH)
    for other in (across, beside):
        pl.semaphore_signal(barrier, inc=1, device_id=(expert, other), device_id_type=pl.DeviceIdType.MESH)
    load1 = pltpu.make_async_copy(w1_hbm.at[0], w1, load_sem.at[0])
    load2 = pltpu.make_async_copy(w2_hbm.at[0], w2, load_sem.at[1])
    load1.start()
    load2.start()

    total = experts * capacity
    row = lax.broadcasted_iota(jnp.int32, (total, in_ref.shape[0]), 0)
    gate = gate_ref[...].astype(f32)
    ones = []
    for k in range(2):
        slot = slots_ref[k : k + 1, :]
        place = jnp.where(slot >= 0, ids_ref[k : k + 1, :] * capacity + slot, total)
        ones.append(jnp.where((place ^ (expert * capacity)) == row, 1.0, 0.0).astype(f32))
    pick[0] = ones[0].astype(bf16)
    pick[1] = ones[1].astype(bf16)
    both = (ones[0] + ones[1]).astype(bf16)
    gates = (ones[0] * gate[0:1, :] + ones[1] * gate[1:2, :]).astype(bf16)
    along = (((0,), (0,)), ((), ()))
    packed[:, 0:width] = jnp.dot(both, in_ref[...], preferred_element_type=f32).astype(bf16)
    packed[:, width : 2 * width] = jnp.dot(both, cot_ref[...], preferred_element_type=f32).astype(bf16)
    packed[:, 2 * width :] = jnp.dot(
        gates, jnp.ones((in_ref.shape[0], pad), bf16), preferred_element_type=f32
    ).astype(bf16)
    slots[at(mine * capacity, capacity, capacity)] = packed[0:capacity]

    pl.semaphore_wait(barrier, experts + 1)
    for d in range(1, experts):
        remote(SEND, d).start()
    remote(ACROSS, 0).start()
    remote(BESIDE, 0).start()

    pairs = experts // 2

    def forward(p):
        for d in (2 * p, 2 * p + 1):
            if d > 0:
                remote(SEND, d).wait_recv()
                remote(ACROSS, d).start()
                remote(BESIDE, d).start()

    def pass_on(p):
        for d in (2 * p, 2 * p + 1):
            remote(ACROSS, d).wait_recv()
            remote(PASS_ON, d).start()

    def compute(p):
        for d in (2 * p, 2 * p + 1):
            remote(BESIDE, d).wait_recv()
            remote(PASS_ON, d).wait_recv()
        span = slice(2 * p * rows, (2 * p + 2) * rows)
        inner[...] = jnp.zeros_like(inner)

        @pl.loop(0, hid // tile)
        def _(n):
            cols = at(n * tile, tile, tile)
            pre = jnp.dot(slots[span, 0:width], w1[:, cols], preferred_element_type=f32)
            back = lax.dot_general(
                slots[span, width : 2 * width], w2[cols, :], (((1,), (1,)), ((), ())),
                preferred_element_type=f32,
            )
            activation, derivative = gelu_pair(pre)
            activation = activation.astype(bf16)
            gate = slots[span, 2 * width :].astype(f32)[:, 0:1]
            act[span, cols] = activation
            hidden[span, cols] = (gate * back * derivative).astype(bf16)
            product = activation.astype(f32) * back
            inner[...] += sum(product[:, c : c + pad] for c in range(0, tile, pad))

        gate = slots[span, 2 * width :].astype(f32)[:, 0:1]
        scaled[span, :] = (gate * slots[span, width : 2 * width].astype(f32)).astype(bf16)

        @pl.loop(0, width // tile)
        def _(n):
            cols = at(n * tile, tile, tile)
            part[span, cols] = lax.dot_general(
                hidden[span, :], w1[cols, :], (((1,), (1,)), ((), ())), preferred_element_type=f32
            ).astype(bf16)

        part[span, width:] = jnp.broadcast_to(
            jnp.sum(inner[...], axis=1, keepdims=True), inner.shape
        ).astype(bf16)
        for d in (2 * p, 2 * p + 1):
            remote(ADD_BESIDE, d).start()

    def chip_sum(d, x):
        return (
            part[at(d * rows + (core * 2 + x) * capacity, capacity, capacity)].astype(f32)
            + got_beside[at(d * 2 * capacity + x * capacity, capacity, capacity)].astype(f32)
        )

    def add_across(p):
        for d in (2 * p, 2 * p + 1):
            remote(ADD_BESIDE, d).wait_recv()
            to_across[d * capacity : (d + 1) * capacity] = chip_sum(d, 1 - half).astype(bf16)
            remote(ADD_ACROSS, d).start()

    def give_back(p):
        for d in (2 * p, 2 * p + 1):
            span = slice(d * capacity, (d + 1) * capacity)
            remote(ADD_ACROSS, d).wait_recv()
            whole = (chip_sum(d, half) + got_across[span].astype(f32)).astype(bf16)
            if d == 0:
                got_return[span] = whole
            else:
                to_return[span] = whole
                remote(RETURN, d).start()

    def weight_tile(which, n):
        cols = at(n * tile, tile, tile)
        if which == 0:
            dw1[cols, :] = lax.dot_general(
                slots[:, cols], hidden[...], along, preferred_element_type=f32
            ).astype(bf16)
        else:
            dw2[cols, :] = lax.dot_general(
                act[:, cols], scaled[...], along, preferred_element_type=f32
            ).astype(bf16)

    def weight_grad(which):
        @pl.loop(0, (width if which == 0 else hid) // tile)
        def _(n):
            weight_tile(which, n)

        store = pltpu.make_async_copy(
            (dw1, dw2)[which], (dw1_hbm, dw2_hbm)[which].at[0], store_sem.at[which]
        )
        store.start()
        return store

    forward(0)
    if pairs > 1:
        forward(1)
    pass_on(0)
    load1.wait()
    load2.wait()
    for p in range(pairs):
        compute(p)
        if p + 2 < pairs:
            forward(p + 2)
        add_across(p)
        if p + 1 < pairs:
            pass_on(p + 1)
        if p >= 1:
            give_back(p - 1)
    store1 = weight_grad(0)
    give_back(pairs - 1)
    store2 = weight_grad(1)

    for d in range(1, experts):
        remote(RETURN, d).wait_recv()
    both = pick[0] + pick[1]
    dx_ref[...] = lax.dot_general(
        both, got_return[:, 0:width], along, preferred_element_type=f32
    ).astype(bf16)
    sides = [
        lax.dot_general(got_return[:, width:], pick[k], along, preferred_element_type=f32)[0:2]
        for k in range(2)
    ]
    side = lax.broadcasted_iota(jnp.int32, sides[0].shape, 0)
    dgate_ref[...] = jnp.where(side == 0, sides[0], sides[1]).astype(bf16)

    for d in range(experts):
        for kind in range(7):
            if d > 0 or kind not in (SEND, RETURN):
                remote(kind, d).wait_send()
    store1.wait()
    store2.wait()


def hand_over_kernel(pieces, *refs):
    count = len(pieces)
    sources, results, held = refs[:count], refs[count : 2 * count], refs[2 * count : 3 * count]
    load_sem, store_sem = refs[3 * count :]
    moves = []
    for i, split in enumerate(pieces):
        height = sources[i].shape[0] // split
        for j in range(split):
            part = pl.ds(j * height, height)
            n = len(moves)
            moves.append((
                pltpu.make_async_copy(sources[i].at[part], held[i].at[part], load_sem.at[n]),
                pltpu.make_async_copy(held[i].at[part], results[i].at[part], store_sem.at[n]),
            ))
    for load, _ in moves:
        load.start()
    for load, store in moves:
        load.wait()
        store.start()
    for _, store in moves:
        store.wait()


def hand_over(arrays, pieces):
    hbm = pl.BlockSpec(memory_space=pl.ANY)
    shapes = tuple(jax.ShapeDtypeStruct(a.shape, a.dtype) for a in arrays)
    return pl.pallas_call(
        functools.partial(hand_over_kernel, pieces),
        out_shape=shapes,
        in_specs=[hbm] * len(arrays),
        out_specs=(hbm,) * len(arrays),
        scratch_shapes=[pltpu.VMEM(a.shape, a.dtype) for a in arrays]
        + [pltpu.SemaphoreType.DMA((sum(pieces),))] * 2,
        compiler_params=pltpu.CompilerParams(vmem_limit_bytes=56 * 1024 * 1024),
    )(*arrays)


def fused(inputs, out_grad, expert_ids, slot_ids, gate_values, first_layer, second_layer):
    experts = lax.axis_size("expert")
    tokens, width = inputs.shape
    capacity = expert_ids.shape[1] * tokens // experts
    hid = first_layer.shape[2]
    total = experts * capacity
    bf16, f32 = jnp.bfloat16, jnp.float32
    vmem = pl.BlockSpec(memory_space=pltpu.VMEM)
    hbm = pl.BlockSpec(memory_space=pl.ANY)
    flops = 10 * 4 * total * width * hid
    dx, dgate, dw1, dw2 = pl.pallas_call(
        functools.partial(fused_kernel, experts, capacity),
        out_shape=(
            jax.ShapeDtypeStruct(inputs.shape, bf16),
            jax.ShapeDtypeStruct(gate_values.shape[::-1], bf16),
            jax.ShapeDtypeStruct(first_layer.shape, bf16),
            jax.ShapeDtypeStruct(second_layer.shape, bf16),
        ),
        in_specs=[vmem] * 5 + [hbm] * 2,
        out_specs=(vmem, vmem, hbm, hbm),
        scratch_shapes=[
            pltpu.VMEM((width, hid), bf16),
            pltpu.VMEM((hid, width), bf16),
            pltpu.VMEM((2, total, tokens), bf16),
            pltpu.VMEM((total, 2 * width + 128), bf16),
            pltpu.VMEM((4 * total, 2 * width + 128), bf16),
            pltpu.VMEM((4 * total, hid), bf16),
            pltpu.VMEM((4 * total, hid), bf16),
            pltpu.VMEM((4 * total, width), bf16),
            pltpu.VMEM((8 * capacity, 128), f32),
            pltpu.VMEM((4 * total, width + 128), bf16),
            pltpu.VMEM((2 * total, width + 128), bf16),
            pltpu.VMEM((total, width + 128), bf16),
            pltpu.VMEM((total, width + 128), bf16),
            pltpu.VMEM((total, width + 128), bf16),
            pltpu.VMEM((total, width + 128), bf16),
            pltpu.VMEM((width, hid), bf16),
            pltpu.VMEM((hid, width), bf16),
            pltpu.SemaphoreType.DMA((7, experts)),
            pltpu.SemaphoreType.DMA((7, experts)),
            pltpu.SemaphoreType.DMA((2,)),
            pltpu.SemaphoreType.DMA((2,)),
        ],
        compiler_params=pltpu.CompilerParams(
            collective_id=0, has_side_effects=True, vmem_limit_bytes=56 * 1024 * 1024
        ),
        cost_estimate=pl.CostEstimate(flops=flops, bytes_accessed=16 * width * hid, transcendentals=4 * total * hid),
    )(inputs, out_grad, expert_ids.T, slot_ids.T, gate_values.T, first_layer, second_layer)
    first_grad, second_grad, dx, dgate = hand_over((dw1[0], dw2[0], dx, dgate), (4, 4, 1, 1))
    return dx, dgate.T, first_grad[None], second_grad[None]


def solution(mesh):
    placed = (
        P(("expert", "dp"), None),
        P(("expert", "dp"), None),
        P(("expert", "dp"), None),
        P(("expert", "dp"), None),
        P(("expert", "dp"), None),
        P("expert", None, "dp"),
        P("expert", "dp", None),
    )
    experts = mesh.shape["expert"]

    def chosen(inputs, out_grad, expert_ids, *rest):
        capacity = expert_ids.shape[1] * inputs.shape[0] // experts
        fits = capacity % 16 == 0 and experts & (experts - 1) == 0 and experts > 1
        fits = fits and mesh.shape["dp"] == 4 and capacity & (capacity - 1) == 0
        return (fused if fits else per_device)(inputs, out_grad, expert_ids, *rest)

    return jax.shard_map(
        chosen,
        mesh=mesh,
        in_specs=placed,
        out_specs=(
            P(("expert", "dp"), None),
            P(("expert", "dp"), None),
            P("expert", None, "dp"),
            P("expert", "dp", None),
        ),
        check_vma=False,
    )
```
